32 devices in a mesh: wa: 2 (over core), ha: 16 (over z, y, x).
Axes of the slice: x: 2, y: 2, z: 4, core: 2. Of those that a mesh axis runs over, the one named last changes fastest.
Arguments:
- tokens: bfloat16 [256, 16384], P('ha', 'wa'), may hold values from -6 to 6
- cotangent: bfloat16 [256, 16384], P('ha', 'wa'), may hold values from -6 to 6
- gate_weight: bfloat16 [16384, 12288], P('wa', 'ha'), may hold values from -0.046875 to 0.046875
- up_weight: bfloat16 [16384, 12288], P('wa', 'ha'), may hold values from -0.046875 to 0.046875
- down_weight: bfloat16 [12288, 16384], P('ha', 'wa'), may hold values from -0.0546875 to 0.0546875
Outputs:
- input_grad: bfloat16 [256, 16384], P('ha', 'wa')
- gate_weight_grad: bfloat16 [16384, 12288], P('wa', 'ha')
- up_weight_grad: bfloat16 [16384, 12288], P('wa', 'ha')
- down_weight_grad: bfloat16 [12288, 16384], P('ha', 'wa')
The draws below stay inside these ranges and needn't reach their ends.
All inputs are finite; a program needn't handle non-finite values.
Results may differ from the reference program's by a relative error of at most 0.0049.
Values may be sent and summed in bfloat16 or wider, within the bound.
A program may use at most 192 MiB of HBM per device.

```python
import jax
import jax.numpy as jnp
from jax import lax

D = 16384
FF = 12288
TOKENS = 256


def shard_levels(rng, dims, split, low, high):
    def one(position, parts):
        heights = jax.random.uniform(jax.random.fold_in(jax.random.fold_in(rng, 6), position), (parts,), jnp.float32, low / len(split), high / len(split))
        return jnp.repeat(jnp.exp(heights), dims[position] // parts).reshape((-1,) + (1,) * (len(dims) - position - 1))

    gain = one(*split[0])
    for cut in split[1:]:
        gain = gain * one(*cut)
    return gain


def scatter_about(stream_key, dims, spread, most, split=(), kind=jnp.bfloat16):
    loudness = shard_levels(stream_key, dims, split, -0.22, 0.18) if split else 1.0
    array = jax.random.normal(stream_key, dims, jnp.float32) * spread * loudness
    return jnp.minimum(jnp.maximum(array, -most), most).astype(kind)


def setup_inputs(seed: int = 0) -> dict:
    splits = jax.random.split(jax.random.key(seed), 6)
    tokens = scatter_about(splits[0], (TOKENS, D), 1.0, 6.0, ((0, 16), (1, 2)))
    cotangent = scatter_about(splits[1], (TOKENS, D), 1.0, 6.0, ((0, 16), (1, 2)))
    gate_weight = scatter_about(splits[2], (D, FF), D ** -0.5, 0.046875, ((0, 2), (1, 16)))
    up_weight = scatter_about(splits[3], (D, FF), D ** -0.5, 0.046875, ((0, 2), (1, 16)))
    down_weight = scatter_about(splits[4], (FF, D), FF ** -0.5, 0.0546875, ((0, 16), (1, 2)))
    return dict(tokens=tokens, cotangent=cotangent, gate_weight=gate_weight, up_weight=up_weight, down_weight=down_weight)


def reference(tokens, cotangent, gate_weight, up_weight, down_weight):
    factor = TOKENS ** -0.5
    gate_sum = jnp.dot(tokens, gate_weight, preferred_element_type=jnp.float32)
    up_sum = jnp.dot(tokens, up_weight, preferred_element_type=jnp.float32)
    hidden_grad = lax.dot_general(cotangent, down_weight, (((1,), (1,)), ((), ())), preferred_element_type=jnp.float32)
    sigma = jax.nn.sigmoid(gate_sum)
    hidden = (gate_sum * sigma * up_sum).astype(jnp.bfloat16)
    gate_grad = (hidden_grad * up_sum * sigma * (1.0 + gate_sum * (1.0 - sigma))).astype(jnp.bfloat16)
    up_grad = (hidden_grad * gate_sum * sigma).astype(jnp.bfloat16)
    down_weight_grad = (lax.dot_general(hidden, cotangent, (((0,), (0,)), ((), ())), preferred_element_type=jnp.float32) * factor).astype(jnp.bfloat16)
    gate_weight_grad = (lax.dot_general(tokens, gate_grad, (((0,), (0,)), ((), ())), preferred_element_type=jnp.float32) * factor).astype(jnp.bfloat16)
    up_weight_grad = (lax.dot_general(tokens, up_grad, (((0,), (0,)), ((), ())), preferred_element_type=jnp.float32) * factor).astype(jnp.bfloat16)
    input_grad = lax.dot_general(gate_grad, gate_weight, (((1,), (1,)), ((), ())), preferred_element_type=jnp.float32)
    input_grad = input_grad + lax.dot_general(up_grad, up_weight, (((1,), (1,)), ((), ())), preferred_element_type=jnp.float32)
    return input_grad.astype(jnp.bfloat16), gate_weight_grad, up_weight_grad, down_weight_grad
```

```python
import functools
import itertools

import jax
import jax.numpy as jnp
from jax import lax
from jax.experimental import pallas as pl
from jax.experimental.pallas import tpu as pltpu
from jax.sharding import PartitionSpec as P

MESH = pl.DeviceIdType.MESH
BF16, F32 = jnp.bfloat16, jnp.float32
VMEM_LIMIT = 60 * 1024 * 1024

GATHER_PARTS = ((0, 7, (0, 1, 2)), (7, 7, (0, 2, 1)), (14, 1, (2, 1, 0)), (15, 1, (1, 2, 0)))
SUM_PARTS = (
    (0, 4, (2, 1, 0)),
    (7, 4, (1, 2, 0)),
    (14, 1, (0, 1, 2)),
    (15, 1, (0, 2, 1)),
    (4, 3, (2, 1, 0)),
    (11, 3, (1, 2, 0)),
)


def pointwise(gate_sum, up_sum, hidden_grad):
    sigma = jax.nn.sigmoid(gate_sum)
    hidden = (gate_sum * sigma * up_sum).astype(BF16)
    gate_grad = (hidden_grad * up_sum * sigma * (1.0 + gate_sum * (1.0 - sigma))).astype(BF16)
    up_grad = (hidden_grad * gate_sum * sigma).astype(BF16)
    return (hidden, gate_grad, up_grad)


def contract_rows(left, right):
    return lax.dot_general(left, right, (((0,), (0,)), ((), ())), preferred_element_type=F32)


def contract_cols(left, right):
    return lax.dot_general(left, right, (((1,), (1,)), ((), ())), preferred_element_type=F32)


def main_kernel(
    dims, cores,
    tok_ref, cot_ref, wg_ref, wu_ref, wd_ref,
    xall_ref, gall_ref, hidden_ref, gg_ref, ug_ref, out_ref,
    x_buf, g_buf, wg, wu, wd, part, wa_recv, rs_recv,
    in_sem, w_sem, copy_sem, ag_send, ag_recv, wa_send, wa_recv_sem, rs_send, rs_sem,
):
    rows, width = tok_ref.shape
    ff = wg_ref.shape[1]
    tokens = rows * dims[0] * dims[1] * dims[2]
    unit = width // 16
    ha = lax.axis_index("ha")
    core = lax.axis_index("wa")
    me = (
        lax.div(ha, dims[1] * dims[2]),
        lax.rem(lax.div(ha, dims[2]), dims[1]),
        lax.rem(ha, dims[2]),
    )

    def moved(at, axis, by):
        pos = list(at)
        pos[axis] = lax.rem(at[axis] + by + dims[axis], dims[axis])
        return tuple(pos)

    def index(at):
        return (at[0] * dims[1] + at[1]) * dims[2] + at[2]

    def origin(kid):
        return tuple(lax.rem(me[a] - kid[a] + dims[a], dims[a]) for a in range(3))

    barrier = pltpu.get_barrier_semaphore()
    greeted = 0
    for axis in range(3):
        for by in range(1, dims[axis]):
            pl.semaphore_signal(
                barrier, inc=1, device_id={"ha": index(moved(me, axis, by))}, device_id_type=MESH
            )
            greeted += 1
    for by in range(1, cores):
        pl.semaphore_signal(
            barrier, inc=1, device_id={"wa": lax.rem(core + by, cores)}, device_id_type=MESH
        )
        greeted += 1

    bufs = (x_buf, g_buf)
    own = [
        pltpu.make_async_copy(ref, buf.at[me[0], me[1], me[2]], in_sem.at[i])
        for i, (ref, buf) in enumerate(((tok_ref, x_buf), (cot_ref, g_buf)))
    ]
    for copy in own:
        copy.start()
    loads = [
        pltpu.make_async_copy(ref, buf, w_sem.at[i])
        for i, (ref, buf) in enumerate(((wg_ref, wg), (wu_ref, wu), (wd_ref, wd)))
    ]
    pl.semaphore_wait(barrier, greeted)

    def sem_id(arr, p, kid):
        return ((arr * len(GATHER_PARTS) + p) * dims[0] + kid[0]) * dims[1] * dims[2] + (
            kid[1] * dims[2] + kid[2]
        )

    sends = {0: [], 1: []}

    def shard(arr, p, kid):
        start, size, _ = GATHER_PARTS[p]
        at = origin(kid)
        return bufs[arr].at[at[0], at[1], at[2], :, pl.ds(start * unit, size * unit)]

    def forward(arr, p, kid, axis):
        for by in range(1, dims[axis]):
            there = list(kid)
            there[axis] += by
            ref = shard(arr, p, kid)
            copy = pltpu.make_async_remote_copy(
                src_ref=ref, dst_ref=ref,
                send_sem=ag_send.at[sem_id(arr, p, there)],
                recv_sem=ag_recv.at[sem_id(arr, p, there)],
                device_id={"ha": index(moved(me, axis, by))}, device_id_type=MESH,
            )
            copy.start()
            sends[arr].append(copy)

    def arrived(arr, p, kid):
        ref = shard(arr, p, kid)
        pltpu.make_async_remote_copy(
            src_ref=ref, dst_ref=ref,
            send_sem=ag_send.at[sem_id(arr, p, kid)], recv_sem=ag_recv.at[sem_id(arr, p, kid)],
            device_id={"ha": ha}, device_id_type=MESH,
        ).wait_recv()

    every = list(itertools.product(*(range(n) for n in dims)))

    def gather_stage(arr, stage):
        if stage == 0:
            own[arr].wait()
        for p, (_, _, order) in enumerate(GATHER_PARTS):
            for kid in every:
                if stage == 0:
                    take = not any(kid)
                else:
                    take = kid[order[stage - 1]] and not any(kid[a] for a in order[stage:])
                if not take:
                    continue
                if stage:
                    arrived(arr, p, kid)
                for axis in order[stage:]:
                    forward(arr, p, kid, axis)

    depth = min(width, 2048)

    def project(which, lhs, rhs, transposed):
        def block(i):
            cols = pl.ds(pl.multiple_of(i * depth, depth), depth)
            left = lhs[:, :, :, :, cols].reshape(tokens, depth)
            if transposed:
                return contract_cols(left, rhs[:, cols])
            return jnp.dot(left, rhs[cols, :], preferred_element_type=F32)

        part[which] = block(0)

        @pl.loop(1, width // depth)
        def _(i):
            part[which] += block(i)

    wa_copies = []

    def exchange(which):
        for by in range(1, cores):
            copy = pltpu.make_async_remote_copy(
                src_ref=part.at[which], dst_ref=wa_recv.at[by - 1, which],
                send_sem=wa_send.at[by - 1, which], recv_sem=wa_recv_sem.at[by - 1, which],
                device_id={"wa": lax.rem(core + by, cores)}, device_id_type=MESH,
            )
            copy.start()
            wa_copies.append(copy)

    gather_stage(0, 0)
    for load in loads:
        load.start()
    gather_stage(0, 1)
    gather_stage(1, 0)
    gather_stage(0, 2)
    gather_stage(1, 1)
    gather_stage(0, 3)
    x_out = pltpu.make_async_copy(x_buf, xall_ref, copy_sem.at[0])
    x_out.start()
    loads[0].wait()
    project(0, x_buf, wg, False)
    exchange(0)
    gather_stage(1, 2)
    loads[1].wait()
    project(1, x_buf, wu, False)
    exchange(1)
    gather_stage(1, 3)
    g_out = pltpu.make_async_copy(g_buf, gall_ref, copy_sem.at[1])
    g_out.start()
    loads[2].wait()
    project(2, g_buf, wd, True)
    exchange(2)
    x_out.wait()
    for copy in sends[0]:
        copy.wait_send()
    for copy in wa_copies:
        copy.wait()

    slab = 16

    @pl.loop(0, tokens // slab)
    def _(i):
        at = pl.ds(pl.multiple_of(i * slab, slab), slab)
        sums = []
        for which in range(3):
            total = part[which, at, :]
            for by in range(1, cores):
                total = total + wa_recv[by - 1, which, at, :]
            sums.append(total)
        hidden_ref[at, :], gg_ref[at, :], ug_ref[at, :] = pointwise(*sums)

    mine = x_buf
    rs_sends = []

    def spans(p):
        start, size, order = SUM_PARTS[p]
        return start * unit, size * unit, order

    def region(buf, p, order, stage, axis_pos):
        start, size, _ = spans(p)
        at = [slice(None)] * 3
        for a in order[:stage]:
            at[a] = me[a]
        at[order[stage]] = axis_pos
        return buf.at[at[0], at[1], at[2], :, pl.ds(start, size)]

    most = max(dims)

    def sum_send(p, stage):
        _, _, order = spans(p)
        axis = order[stage]
        for by in range(1, dims[axis]):
            there = moved(me, axis, by)
            sem = (p * 3 + stage) * most + by
            copy = pltpu.make_async_remote_copy(
                src_ref=region(mine, p, order, stage, there[axis]),
                dst_ref=region(rs_recv, p, order, stage, me[axis]),
                send_sem=rs_send.at[sem], recv_sem=rs_sem.at[sem],
                device_id={"ha": index(there)}, device_id_type=MESH,
            )
            copy.start()
            rs_sends.append(copy)

    def sum_take(p, stage):
        start, size, order = spans(p)
        axis = order[stage]
        froms = []
        for by in range(1, dims[axis]):
            source = moved(me, axis, -by)
            sem = (p * 3 + stage) * most + by
            ref = region(rs_recv, p, order, stage, source[axis])
            pltpu.make_async_remote_copy(
                src_ref=ref, dst_ref=ref, send_sem=rs_send.at[sem], recv_sem=rs_sem.at[sem],
                device_id={"ha": ha}, device_id_type=MESH,
            ).wait_recv()
            froms.append(source[axis])
        left = [a for a in range(3) if a not in order[: stage + 1]]
        count = 1
        for a in left:
            count *= dims[a]
        cols = pl.ds(start, size)

        def one(i):
            at = [None] * 3
            for a in order[: stage + 1]:
                at[a] = me[a]
            rest = i
            for a in reversed(left):
                at[a] = lax.rem(rest, dims[a])
                rest = lax.div(rest, dims[a])
            total = mine[at[0], at[1], at[2], :, cols].astype(F32)
            for source in froms:
                pos = list(at)
                pos[axis] = source
                total = total + rs_recv[pos[0], pos[1], pos[2], :, cols].astype(F32)
            if left:
                mine[at[0], at[1], at[2], :, cols] = total.astype(BF16)
            else:
                out_ref[:, cols] = total.astype(BF16)

        if left:
            pl.loop(0, count)(one)
        else:
            one(0)

    for p in range(len(SUM_PARTS)):
        start, size, _ = SUM_PARTS[p]

        @pl.loop(start, start + size)
        def _(i):
            cols = pl.ds(pl.multiple_of(i * unit, unit), unit)
            total = contract_cols(gg_ref[...], wg[cols, :]) + contract_cols(ug_ref[...], wu[cols, :])
            mine[:, :, :, :, cols] = total.astype(BF16).reshape(*dims, rows, unit)

        sum_send(p, 0)
    for stage in range(3):
        for p in range(len(SUM_PARTS)):
            sum_take(p, stage)
            if stage < 2:
                sum_send(p, stage + 1)
    for copy in rs_sends + sends[1]:
        copy.wait_send()
    g_out.wait()


def weight_kernel(factor, x_ref, g_ref, hidden_ref, gg_ref, ug_ref, dgate_ref, dup_ref, ddown_ref):
    tokens = hidden_ref.shape[0]
    x = x_ref[...].reshape(tokens, x_ref.shape[-1])
    g = g_ref[...].reshape(tokens, g_ref.shape[-1])
    dgate_ref[...] = (contract_rows(x, gg_ref[...]) * factor).astype(BF16)
    dup_ref[...] = (contract_rows(x, ug_ref[...]) * factor).astype(BF16)
    ddown_ref[...] = (contract_rows(hidden_ref[...], g) * factor).astype(BF16)


def weight_grads(x_all, g_all, hidden, gate_grad, up_grad, factor):
    lead, width = x_all.shape[:-1], x_all.shape[-1]
    tokens, ff = hidden.shape
    step = 512
    gathered = pl.BlockSpec((*lead, step), lambda i: (0, 0, 0, 0, i))
    whole = pl.BlockSpec((tokens, ff), lambda i: (0, 0))
    tall = pl.BlockSpec((step, ff), lambda i: (i, 0))
    return pl.pallas_call(
        functools.partial(weight_kernel, factor),
        grid=(width // step,),
        out_shape=(
            jax.ShapeDtypeStruct((width, ff), BF16),
            jax.ShapeDtypeStruct((width, ff), BF16),
            jax.ShapeDtypeStruct((ff, width), BF16),
        ),
        in_specs=[gathered, gathered, whole, whole, whole],
        out_specs=(tall, tall, pl.BlockSpec((ff, step), lambda i: (0, i))),
        compiler_params=pltpu.CompilerParams(vmem_limit_bytes=VMEM_LIMIT),
        cost_estimate=pl.CostEstimate(
            flops=6 * tokens * ff * width, bytes_accessed=2 * width * (3 * ff + 2 * tokens),
            transcendentals=0,
        ),
    )(x_all, g_all, hidden, gate_grad, up_grad)


def on_device(dims, cores, tokens, cotangent, gate_weight, up_weight, down_weight):
    rows, width = tokens.shape
    ff = gate_weight.shape[1]
    count = rows * dims[0] * dims[1] * dims[2]
    shards = dims[0] * dims[1] * dims[2]
    gathered = (*dims, rows, width)
    hbm = pl.BlockSpec(memory_space=pl.ANY)
    vmem = pl.BlockSpec(memory_space=pltpu.VMEM)
    dma = pltpu.SemaphoreType.DMA
    ag_count = 2 * len(GATHER_PARTS) * shards
    rs_count = 3 * len(SUM_PARTS) * max(dims)
    others = max(cores - 1, 1)
    x_all, g_all, hidden, gate_grad, up_grad, input_grad = pl.pallas_call(
        functools.partial(main_kernel, dims, cores),
        out_shape=(
            jax.ShapeDtypeStruct(gathered, BF16),
            jax.ShapeDtypeStruct(gathered, BF16),
            jax.ShapeDtypeStruct((count, ff), BF16),
            jax.ShapeDtypeStruct((count, ff), BF16),
            jax.ShapeDtypeStruct((count, ff), BF16),
            jax.ShapeDtypeStruct((rows, width), BF16),
        ),
        in_specs=[hbm] * 5,
        out_specs=(hbm, hbm, vmem, vmem, vmem, vmem),
        scratch_shapes=[
            pltpu.VMEM(gathered, BF16),
            pltpu.VMEM(gathered, BF16),
            pltpu.VMEM((width, ff), BF16),
            pltpu.VMEM((width, ff), BF16),
            pltpu.VMEM((ff, width), BF16),
            pltpu.VMEM((3, count, ff), F32),
            pltpu.VMEM((others, 3, count, ff), F32),
            pltpu.VMEM(gathered, BF16),
            dma((2,)), dma((3,)), dma((2,)),
            dma((ag_count,)), dma((ag_count,)),
            dma((others, 3)), dma((others, 3)),
            dma((rs_count,)), dma((rs_count,)),
        ],
        compiler_params=pltpu.CompilerParams(
            collective_id=0, has_side_effects=True, vmem_limit_bytes=VMEM_LIMIT
        ),
        cost_estimate=pl.CostEstimate(
            flops=10 * count * ff * width, bytes_accessed=2 * width * (3 * ff + 2 * count),
            transcendentals=count * ff,
        ),
    )(tokens, cotangent, gate_weight, up_weight, down_weight)
    grads = weight_grads(x_all, g_all, hidden, gate_grad, up_grad, count ** (-0.5))
    return (input_grad, *grads)


def on_device_plain(tokens, cotangent, gate_weight, up_weight, down_weight):
    inputs_all = lax.all_gather(tokens, "ha", axis=0, tiled=True)
    grads_all = lax.all_gather(cotangent, "ha", axis=0, tiled=True)
    factor = inputs_all.shape[0] ** (-0.5)
    gate_part = jnp.dot(inputs_all, gate_weight, preferred_element_type=F32)
    up_part = jnp.dot(inputs_all, up_weight, preferred_element_type=F32)
    hidden_part = contract_cols(grads_all, down_weight)
    gate_sum, up_sum, hidden_grad = lax.psum((gate_part, up_part, hidden_part), "wa")
    hidden, gate_grad, up_grad = pointwise(gate_sum, up_sum, hidden_grad)
    down_weight_grad = (contract_rows(hidden, grads_all) * factor).astype(BF16)
    gate_weight_grad = (contract_rows(inputs_all, gate_grad) * factor).astype(BF16)
    up_weight_grad = (contract_rows(inputs_all, up_grad) * factor).astype(BF16)
    input_grad = lax.psum_scatter(
        contract_cols(gate_grad, gate_weight) + contract_cols(up_grad, up_weight),
        "ha", scatter_dimension=0, tiled=True,
    )
    return (input_grad.astype(BF16), gate_weight_grad, up_weight_grad, down_weight_grad)


def fits(dims, cores, rows, width, ff):
    count = dims[0] * dims[1] * dims[2] * rows
    held = 6 * count * width + 6 * width * ff + 12 * cores * count * ff + 6 * count * ff
    return rows % 16 == 0 and width % 2048 == 0 and ff % 128 == 0 and held < VMEM_LIMIT


def solution(mesh):
    placed = (P("ha", "wa"), P("ha", "wa"), P("wa", "ha"), P("wa", "ha"), P("ha", "wa"))
    cores, along = mesh.shape["wa"], mesh.shape["ha"]
    dims = (along // 4, 2, 2) if along % 4 == 0 else (along, 1, 1)

    def body(tokens, cotangent, gate_weight, up_weight, down_weight):
        plan = on_device_plain
        if fits(dims, cores, *tokens.shape, gate_weight.shape[1]):
            plan = functools.partial(on_device, dims, cores)
        return plan(tokens, cotangent, gate_weight, up_weight, down_weight)

    return jax.shard_map(
        body,
        mesh=mesh,
        in_specs=placed,
        out_specs=(P("ha", "wa"), P("wa", "ha"), P("wa", "ha"), P("ha", "wa")),
        check_vma=False,
    )
```

```python
import functools
import itertools

import jax
import jax.numpy as jnp
from jax import lax
from jax.experimental import pallas as pl
from jax.experimental.pallas import tpu as pltpu
from jax.sharding import PartitionSpec as P

MESH = pl.DeviceIdType.MESH
BF16, F32 = jnp.bfloat16, jnp.float32
VMEM_LIMIT = 61 * 1024 * 1024

GATHER_PARTS = ((0, 26, (0, 1, 2)), (26, 26, (0, 2, 1)), (52, 6, (2, 1, 0)), (58, 6, (1, 2, 0)))
SUM_PARTS = (
    (0, 4, (0, 1, 2)),
    (4, 4, (0, 2, 1)),
    (8, 8, (2, 1, 0)),
    (16, 8, (1, 2, 0)),
    (24, 8, (2, 1, 0)),
    (32, 8, (1, 2, 0)),
    (40, 8, (2, 1, 0)),
    (48, 8, (1, 2, 0)),
    (56, 4, (2, 1, 0)),
    (60, 4, (1, 2, 0)),
)
SUM_WAVES = ((0, 1, 2, 3), (4, 5), (6, 7), (8, 9))


def pointwise(gate_sum, up_sum, hidden_grad):
    sigma = jax.nn.sigmoid(gate_sum)
    hidden = (gate_sum * sigma * up_sum).astype(BF16)
    gate_grad = (hidden_grad * up_sum * sigma * (1.0 + gate_sum * (1.0 - sigma))).astype(BF16)
    up_grad = (hidden_grad * gate_sum * sigma).astype(BF16)
    return (hidden, gate_grad, up_grad)


def contract_rows(left, right):
    return lax.dot_general(left, right, (((0,), (0,)), ((), ())), preferred_element_type=F32)


def contract_cols(left, right):
    return lax.dot_general(left, right, (((1,), (1,)), ((), ())), preferred_element_type=F32)


def main_kernel(
    dims, cores,
    tok_ref, cot_ref, wg_ref, wu_ref, wd_ref,
    xt_ref, gall_ref, hidden_t_ref, gg_ref, ug_ref, out_ref,
    x_buf, g_buf, wg, wu, wd, part, wa_recv, rs_recv, flip, hidden_buf,
    in_sem, w_sem, copy_sem, ag_send, ag_recv, wa_send, wa_recv_sem, rs_send, rs_sem,
):
    rows, width = tok_ref.shape
    ff = wg_ref.shape[1]
    tokens = rows * dims[0] * dims[1] * dims[2]
    unit = width // 64
    ha = lax.axis_index("ha")
    core = lax.axis_index("wa")
    me = (
        lax.div(ha, dims[1] * dims[2]),
        lax.rem(lax.div(ha, dims[2]), dims[1]),
        lax.rem(ha, dims[2]),
    )

    def moved(at, axis, by):
        pos = list(at)
        pos[axis] = lax.rem(at[axis] + by + dims[axis], dims[axis])
        return tuple(pos)

    def index(at):
        return (at[0] * dims[1] + at[1]) * dims[2] + at[2]

    def origin(kid):
        return (
            me[0] + kid[0],
            lax.rem(me[1] - kid[1] + dims[1], dims[1]),
            lax.rem(me[2] - kid[2] + dims[2], dims[2]),
        )

    def when(conds, run):
        if not conds:
            run()
            return
        ok = conds[0]()
        for cond in conds[1:]:
            ok = jnp.logical_and(ok, cond())
        pl.when(ok)(run)

    def on_line(by):
        return lambda: me[0] + by < dims[0] if by > 0 else me[0] + by >= 0

    def exists(kid):
        return [on_line(kid[0])] if kid[0] else []

    barrier = pltpu.get_barrier_semaphore()
    greeted = 0
    for axis in range(3):
        for by in range(1, dims[axis]):
            pl.semaphore_signal(
                barrier, inc=1, device_id={"ha": index(moved(me, axis, by))}, device_id_type=MESH
            )
            greeted += 1
    for by in range(1, cores):
        pl.semaphore_signal(
            barrier, inc=1, device_id={"wa": lax.rem(core + by, cores)}, device_id_type=MESH
        )
        greeted += 1

    bufs = (x_buf, g_buf)
    own = [
        pltpu.make_async_copy(ref, buf.at[me[0], me[1], me[2]], in_sem.at[i])
        for i, (ref, buf) in enumerate(((tok_ref, x_buf), (cot_ref, g_buf)))
    ]
    for copy in own:
        copy.start()
    loads = [
        pltpu.make_async_copy(ref, buf, w_sem.at[i])
        for i, (ref, buf) in enumerate(((wg_ref, wg), (wu_ref, wu), (wd_ref, wd)))
    ]
    pl.semaphore_wait(barrier, greeted)

    shards = dims[0] * dims[1] * dims[2]

    def recv_sem(arr, p, at):
        return ag_recv.at[(arr * len(GATHER_PARTS) + p) * shards + index(at)]

    sends = {0: [], 1: []}
    slots = itertools.count()

    def shard(arr, p, at):
        start, size, _ = GATHER_PARTS[p]
        return bufs[arr].at[at[0], at[1], at[2], :, pl.ds(start * unit, size * unit)]

    def remote(arr, p, kid, slot, axis, by):
        at = origin(kid)
        target = moved(me, axis, by) if by else me
        ref = shard(arr, p, at)
        return pltpu.make_async_remote_copy(
            src_ref=ref, dst_ref=ref, send_sem=ag_send.at[slot], recv_sem=recv_sem(arr, p, at),
            device_id={"ha": index(target)}, device_id_type=MESH,
        )

    def forward(arr, p, kid, axis):
        if axis == 0:
            steps = [1, -1] if kid[0] == 0 else [-1 if kid[0] > 0 else 1]
        else:
            steps = range(1, dims[axis])
        for by in steps:
            slot = next(slots)
            conds = []
            if axis == 0:
                if dims[0] == 1:
                    continue
                conds = [on_line(by)]
            make = functools.partial(remote, arr, p, kid, slot, axis, by)
            when(conds, lambda: make().start())
            sends[arr].append((exists(kid) + conds, make))

    def handle(arr, p, kid):
        order = GATHER_PARTS[p][2]
        last = max((order.index(a) for a in range(3) if kid[a]), default=-1)

        def run():
            if last >= 0:
                remote(arr, p, kid, 0, 0, 0).wait_recv()
            for j, axis in enumerate(order):
                if j > last or (j == last and axis == 0):
                    forward(arr, p, kid, axis)

        when(exists(kid), run)

    line = [0] + [d for k in range(1, dims[0]) for d in (-k, k)]
    every = list(itertools.product(line, range(dims[1]), range(dims[2])))

    def kind(p, kid):
        order = GATHER_PARTS[p][2]
        last = max((order.index(a) for a in range(3) if kid[a]), default=-1)
        return last, abs(kid[0])

    def gather(arr, last, dist, line_last=None):
        for p, (_, _, order) in enumerate(GATHER_PARTS):
            if line_last is not None and line_last != (order[2] == 0):
                continue
            for kid in every:
                if kind(p, kid) == (last, dist):
                    handle(arr, p, kid)

    def gather_own(arr):
        own[arr].wait()
        gather(arr, -1, 0)

    def gather_begin(arr):
        gather(arr, 0, 0)
        gather(arr, 1, 0)
        for dist in range(1, dims[0]):
            gather(arr, 0, dist)
            if dist < dims[0] - 1:
                gather(arr, 1, dist)
            if dist > 1:
                gather(arr, 2, dist - 1, True)

    def gather_rest(arr):
        if dims[0] > 1:
            gather(arr, 1, dims[0] - 1)

    def gather_end(arr):
        for dist in range(dims[0]):
            gather(arr, 2, dist, False)
        if dims[0] > 1:
            gather(arr, 2, dims[0] - 1, True)

    depth = min(width, 2048)

    def project(which, lhs, rhs, transposed):
        def block(i):
            cols = pl.ds(pl.multiple_of(i * depth, depth), depth)
            left = lhs[:, :, :, :, cols].reshape(tokens, depth)
            if transposed:
                return contract_cols(left, rhs[:, cols])
            return jnp.dot(left, rhs[cols, :], preferred_element_type=F32)

        part[which] = block(0)

        @pl.loop(1, width // depth)
        def _(i):
            part[which] += block(i)

    wa_copies = []

    def exchange(which):
        for by in range(1, cores):
            copy = pltpu.make_async_remote_copy(
                src_ref=part.at[which], dst_ref=wa_recv.at[by - 1, which],
                send_sem=wa_send.at[by - 1, which], recv_sem=wa_recv_sem.at[by - 1, which],
                device_id={"wa": lax.rem(core + by, cores)}, device_id_type=MESH,
            )
            copy.start()
            wa_copies.append(copy)

    flips = width // flip.shape[1]

    def flipped(i):
        return pltpu.make_async_copy(
            flip.at[i % 2], xt_ref.at[pl.ds(i * flip.shape[1], flip.shape[1]), :],
            copy_sem.at[i % 2],
        )

    def transpose_tokens(first, end):
        for i in range(first, end):
            if i >= 2:
                flipped(i - 2).wait()
            left = x_buf[:, :, :, :, pl.ds(i * flip.shape[1], flip.shape[1])]
            flip[i % 2] = left.reshape(tokens, flip.shape[1]).T
            flipped(i).start()

    gather_own(0)
    for load in loads:
        load.start()
    gather_begin(0)
    gather_own(1)
    gather_rest(0)
    gather_begin(1)
    gather_end(0)
    loads[0].wait()
    project(0, x_buf, wg, False)
    exchange(0)
    gather_rest(1)
    loads[1].wait()
    project(1, x_buf, wu, False)
    exchange(1)
    transpose_tokens(0, flips)
    gather_end(1)
    g_out = pltpu.make_async_copy(g_buf, gall_ref, copy_sem.at[2])
    g_out.start()
    loads[2].wait()
    project(2, g_buf, wd, True)
    exchange(2)
    for i in range(max(flips - 2, 0), flips):
        flipped(i).wait()
    for conds, make in sends[0]:
        when(conds, lambda: make().wait_send())
    for copy in wa_copies:
        copy.wait()

    slab = 16

    @pl.loop(0, tokens // slab)
    def _(i):
        at = pl.ds(pl.multiple_of(i * slab, slab), slab)
        sums = []
        for which in range(3):
            total = part[which, at, :]
            for by in range(1, cores):
                total = total + wa_recv[by - 1, which, at, :]
            sums.append(total)
        hidden_buf[at, :], gg_ref[at, :], ug_ref[at, :] = pointwise(*sums)

    mine = x_buf
    rs_sends = []

    def spans(p):
        start, size, order = SUM_PARTS[p]
        return start * unit, size * unit, order

    def region(buf, p, order, stage, axis_pos):
        start, size, _ = spans(p)
        at = [slice(None)] * 3
        for a in order[:stage]:
            at[a] = me[a]
        at[order[stage]] = axis_pos
        return buf.at[at[0], at[1], at[2], :, pl.ds(start, size)]

    most = max(dims)

    def sum_send(p, stage):
        _, _, order = spans(p)
        axis = order[stage]
        for by in range(1, dims[axis]):
            there = moved(me, axis, by)
            sem = (p * 3 + stage) * most + by
            copy = pltpu.make_async_remote_copy(
                src_ref=region(mine, p, order, stage, there[axis]),
                dst_ref=region(rs_recv, p, order, stage, me[axis]),
                send_sem=rs_send.at[sem], recv_sem=rs_sem.at[sem],
                device_id={"ha": index(there)}, device_id_type=MESH,
            )
            copy.start()
            rs_sends.append(copy)

    def sum_take(p, stage):
        start, size, order = spans(p)
        axis = order[stage]
        froms = []
        for by in range(1, dims[axis]):
            source = moved(me, axis, -by)
            sem = (p * 3 + stage) * most + by
            ref = region(rs_recv, p, order, stage, source[axis])
            pltpu.make_async_remote_copy(
                src_ref=ref, dst_ref=ref, send_sem=rs_send.at[sem], recv_sem=rs_sem.at[sem],
                device_id={"ha": ha}, device_id_type=MESH,
            ).wait_recv()
            froms.append(source[axis])
        left = [a for a in range(3) if a not in order[: stage + 1]]
        count = 1
        for a in left:
            count *= dims[a]
        cols = pl.ds(start, size)

        def one(i):
            at = [None] * 3
            for a in order[: stage + 1]:
                at[a] = me[a]
            rest = i
            for a in reversed(left):
                at[a] = lax.rem(rest, dims[a])
                rest = lax.div(rest, dims[a])
            total = mine[at[0], at[1], at[2], :, cols].astype(F32)
            for source in froms:
                pos = list(at)
                pos[axis] = source
                total = total + rs_recv[pos[0], pos[1], pos[2], :, cols].astype(F32)
            if left:
                mine[at[0], at[1], at[2], :, cols] = total.astype(BF16)
            else:
                out_ref[:, cols] = total.astype(BF16)

        if left:
            pl.loop(0, count)(one)
        else:
            one(0)

    block = 4 * unit

    def compute(p):
        start, size, _ = SUM_PARTS[p]

        @pl.loop(start * unit // block, (start + size) * unit // block)
        def _(i):
            cols = pl.ds(pl.multiple_of(i * block, block), block)
            total = contract_cols(gg_ref[...], wg[cols, :]) + contract_cols(ug_ref[...], wu[cols, :])
            mine[:, :, :, :, cols] = total.astype(BF16).reshape(*dims, rows, block)

    def begin(wave):
        for p in SUM_WAVES[wave]:
            compute(p)
            sum_send(p, 0)

    def advance(wave, stage):
        for p in SUM_WAVES[wave]:
            sum_take(p, stage)
            if stage < 2:
                sum_send(p, stage + 1)

    waves = len(SUM_WAVES)
    begin(0)
    begin(1)
    hidden_t_ref[...] = hidden_buf[...].T
    for turn in range(waves + 1):
        if turn < waves:
            advance(turn, 0)
        if turn + 2 < waves:
            begin(turn + 2)
        if turn >= 1:
            advance(turn - 1, 1)
    for wave in range(waves):
        advance(wave, 2)
    for copy in rs_sends:
        copy.wait_send()
    for conds, make in sends[1]:
        when(conds, lambda: make().wait_send())
    g_out.wait()


def weight_kernel(factor, xt_ref, g_ref, ht_ref, gg_ref, ug_ref, dgate_ref, dup_ref, ddown_ref):
    def product(left, right):
        return (jnp.dot(left, right, preferred_element_type=F32) * factor).astype(BF16)

    g = g_ref[...].reshape(ht_ref.shape[1], g_ref.shape[-1])
    dgate_ref[...] = product(xt_ref[...], gg_ref[...])
    dup_ref[...] = product(xt_ref[...], ug_ref[...])
    ddown_ref[...] = product(ht_ref[...], g)


def weight_grads(x_t, g_all, hidden_t, gate_grad, up_grad, factor):
    lead, width = g_all.shape[:-1], g_all.shape[-1]
    tokens, ff = gate_grad.shape
    step = 512
    whole = pl.BlockSpec((tokens, ff), lambda i: (0, 0))
    tall = pl.BlockSpec((step, ff), lambda i: (i, 0))
    return pl.pallas_call(
        functools.partial(weight_kernel, factor),
        grid=(width // step,),
        out_shape=(
            jax.ShapeDtypeStruct((width, ff), BF16),
            jax.ShapeDtypeStruct((width, ff), BF16),
            jax.ShapeDtypeStruct((ff, width), BF16),
        ),
        in_specs=[
            pl.BlockSpec((step, tokens), lambda i: (i, 0)),
            pl.BlockSpec((*lead, step), lambda i: (0, 0, 0, 0, i)),
            pl.BlockSpec((ff, tokens), lambda i: (0, 0)),
            whole,
            whole,
        ],
        out_specs=(tall, tall, pl.BlockSpec((ff, step), lambda i: (0, i))),
        compiler_params=pltpu.CompilerParams(vmem_limit_bytes=VMEM_LIMIT),
        cost_estimate=pl.CostEstimate(
            flops=6 * tokens * ff * width, bytes_accessed=2 * width * (3 * ff + 2 * tokens),
            transcendentals=0,
        ),
    )(x_t, g_all, hidden_t, gate_grad, up_grad)


def on_device(dims, cores, tokens, cotangent, gate_weight, up_weight, down_weight):
    rows, width = tokens.shape
    ff = gate_weight.shape[1]
    count = rows * dims[0] * dims[1] * dims[2]
    shards = dims[0] * dims[1] * dims[2]
    gathered = (*dims, rows, width)
    hbm = pl.BlockSpec(memory_space=pl.ANY)
    vmem = pl.BlockSpec(memory_space=pltpu.VMEM)
    dma = pltpu.SemaphoreType.DMA
    ag_count = 2 * len(GATHER_PARTS) * shards
    rs_count = 3 * len(SUM_PARTS) * max(dims)
    others = max(cores - 1, 1)
    x_t, g_all, hidden_t, gate_grad, up_grad, input_grad = pl.pallas_call(
        functools.partial(main_kernel, dims, cores),
        out_shape=(
            jax.ShapeDtypeStruct((width, count), BF16),
            jax.ShapeDtypeStruct(gathered, BF16),
            jax.ShapeDtypeStruct((ff, count), BF16),
            jax.ShapeDtypeStruct((count, ff), BF16),
            jax.ShapeDtypeStruct((count, ff), BF16),
            jax.ShapeDtypeStruct((rows, width), BF16),
        ),
        in_specs=[hbm] * 5,
        out_specs=(hbm, hbm, vmem, vmem, vmem, vmem),
        scratch_shapes=[
            pltpu.VMEM(gathered, BF16),
            pltpu.VMEM(gathered, BF16),
            pltpu.VMEM((width, ff), BF16),
            pltpu.VMEM((width, ff), BF16),
            pltpu.VMEM((ff, width), BF16),
            pltpu.VMEM((3, count, ff), F32),
            pltpu.VMEM((others, 3, count, ff), F32),
            pltpu.VMEM(gathered, BF16),
            pltpu.VMEM((2, width // 8, count), BF16),
            pltpu.VMEM((count, ff), BF16),
            dma((2,)), dma((3,)), dma((3,)),
            dma((2 * ag_count,)), dma((ag_count,)),
            dma((others, 3)), dma((others, 3)),
            dma((rs_count,)), dma((rs_count,)),
        ],
        compiler_params=pltpu.CompilerParams(
            collective_id=0, has_side_effects=True, vmem_limit_bytes=VMEM_LIMIT
        ),
        cost_estimate=pl.CostEstimate(
            flops=10 * count * ff * width, bytes_accessed=2 * width * (3 * ff + 2 * count),
            transcendentals=count * ff,
        ),
    )(tokens, cotangent, gate_weight, up_weight, down_weight)
    grads = weight_grads(x_t, g_all, hidden_t, gate_grad, up_grad, count ** (-0.5))
    return (input_grad, *grads)


def on_device_plain(tokens, cotangent, gate_weight, up_weight, down_weight):
    inputs_all = lax.all_gather(tokens, "ha", axis=0, tiled=True)
    grads_all = lax.all_gather(cotangent, "ha", axis=0, tiled=True)
    factor = inputs_all.shape[0] ** (-0.5)
    gate_part = jnp.dot(inputs_all, gate_weight, preferred_element_type=F32)
    up_part = jnp.dot(inputs_all, up_weight, preferred_element_type=F32)
    hidden_part = contract_cols(grads_all, down_weight)
    gate_sum, up_sum, hidden_grad = lax.psum((gate_part, up_part, hidden_part), "wa")
    hidden, gate_grad, up_grad = pointwise(gate_sum, up_sum, hidden_grad)
    down_weight_grad = (contract_rows(hidden, grads_all) * factor).astype(BF16)
    gate_weight_grad = (contract_rows(inputs_all, gate_grad) * factor).astype(BF16)
    up_weight_grad = (contract_rows(inputs_all, up_grad) * factor).astype(BF16)
    input_grad = lax.psum_scatter(
        contract_cols(gate_grad, gate_weight) + contract_cols(up_grad, up_weight),
        "ha", scatter_dimension=0, tiled=True,
    )
    return (input_grad.astype(BF16), gate_weight_grad, up_weight_grad, down_weight_grad)


def fits(dims, cores, rows, width, ff):
    count = dims[0] * dims[1] * dims[2] * rows
    held = 6 * count * width + 6 * width * ff + 12 * cores * count * ff + 6 * count * ff
    return rows % 16 == 0 and width % 2048 == 0 and ff % 128 == 0 and held < VMEM_LIMIT


def solution(mesh):
    placed = (P("ha", "wa"), P("ha", "wa"), P("wa", "ha"), P("wa", "ha"), P("ha", "wa"))
    cores, along = mesh.shape["wa"], mesh.shape["ha"]
    dims = (along // 4, 2, 2) if along % 4 == 0 else (along, 1, 1)

    def body(tokens, cotangent, gate_weight, up_weight, down_weight):
        plan = on_device_plain
        if fits(dims, cores, *tokens.shape, gate_weight.shape[1]):
            plan = functools.partial(on_device, dims, cores)
        return plan(tokens, cotangent, gate_weight, up_weight, down_weight)

    return jax.shard_map(
        body,
        mesh=mesh,
        in_specs=placed,
        out_specs=(P("ha", "wa"), P("wa", "ha"), P("wa", "ha"), P("ha", "wa")),
        check_vma=False,
    )
```

```python
import functools
import itertools

import jax
import jax.numpy as jnp
from jax import lax
from jax.experimental import pallas as pl
from jax.experimental.pallas import tpu as pltpu
from jax.sharding import PartitionSpec as P

MESH = pl.DeviceIdType.MESH
BF16, F32 = jnp.bfloat16, jnp.float32
VMEM_LIMIT = 61 * 1024 * 1024

GATHER_PARTS = ((0, 26, (0, 1, 2)), (26, 26, (0, 2, 1)), (52, 6, (2, 1, 0)), (58, 6, (1, 2, 0)))
SUM_PARTS = (
    (0, 4, (0, 1, 2)),
    (4, 4, (0, 2, 1)),
    (8, 8, (2, 1, 0)),
    (16, 8, (1, 2, 0)),
    (24, 8, (2, 1, 0)),
    (32, 8, (1, 2, 0)),
    (40, 8, (2, 1, 0)),
    (48, 8, (1, 2, 0)),
    (56, 4, (2, 1, 0)),
    (60, 4, (1, 2, 0)),
)
SUM_WAVES = ((0, 1, 2, 3), (4, 5), (6, 7), (8, 9))


def pointwise(gate_sum, up_sum, hidden_grad):
    sigma = jax.nn.sigmoid(gate_sum)
    hidden = (gate_sum * sigma * up_sum).astype(BF16)
    gate_grad = (hidden_grad * up_sum * sigma * (1.0 + gate_sum * (1.0 - sigma))).astype(BF16)
    up_grad = (hidden_grad * gate_sum * sigma).astype(BF16)
    return (hidden, gate_grad, up_grad)


def contract_rows(left, right):
    return lax.dot_general(left, right, (((0,), (0,)), ((), ())), preferred_element_type=F32)


def contract_cols(left, right):
    return lax.dot_general(left, right, (((1,), (1,)), ((), ())), preferred_element_type=F32)


def main_kernel(
    dims, cores,
    tok_ref, cot_ref, wg_ref, wu_ref, wd_ref,
    xall_ref, gall_ref, hidden_ref, gg_ref, ug_ref, out_ref,
    x_buf, g_buf, wg, wu, wd, part, wa_recv, rs_recv, hid_t, grads_t,
    in_sem, w_sem, copy_sem, ag_send, ag_recv, wa_send, wa_recv_sem, rs_send, rs_sem,
):
    rows, width = tok_ref.shape
    ff = wg_ref.shape[1]
    tokens = rows * dims[0] * dims[1] * dims[2]
    unit = width // 64
    ha = lax.axis_index("ha")
    core = lax.axis_index("wa")
    me = (
        lax.div(ha, dims[1] * dims[2]),
        lax.rem(lax.div(ha, dims[2]), dims[1]),
        lax.rem(ha, dims[2]),
    )

    def moved(at, axis, by):
        pos = list(at)
        pos[axis] = lax.rem(at[axis] + by + dims[axis], dims[axis])
        return tuple(pos)

    def index(at):
        return (at[0] * dims[1] + at[1]) * dims[2] + at[2]

    def origin(kid):
        return (
            me[0] + kid[0],
            lax.rem(me[1] - kid[1] + dims[1], dims[1]),
            lax.rem(me[2] - kid[2] + dims[2], dims[2]),
        )

    def when(conds, run):
        if not conds:
            run()
            return
        ok = conds[0]()
        for cond in conds[1:]:
            ok = jnp.logical_and(ok, cond())
        pl.when(ok)(run)

    def on_line(by):
        return lambda: me[0] + by < dims[0] if by > 0 else me[0] + by >= 0

    def exists(kid):
        return [on_line(kid[0])] if kid[0] else []

    barrier = pltpu.get_barrier_semaphore()
    greeted = 0
    for axis in range(3):
        for by in range(1, dims[axis]):
            pl.semaphore_signal(
                barrier, inc=1, device_id={"ha": index(moved(me, axis, by))}, device_id_type=MESH
            )
            greeted += 1
    for by in range(1, cores):
        pl.semaphore_signal(
            barrier, inc=1, device_id={"wa": lax.rem(core + by, cores)}, device_id_type=MESH
        )
        greeted += 1

    bufs = (x_buf, g_buf)
    own = [
        pltpu.make_async_copy(ref, buf.at[me[0], me[1], me[2]], in_sem.at[i])
        for i, (ref, buf) in enumerate(((tok_ref, x_buf), (cot_ref, g_buf)))
    ]
    for copy in own:
        copy.start()
    loads = [
        pltpu.make_async_copy(ref, buf, w_sem.at[i])
        for i, (ref, buf) in enumerate(((wg_ref, wg), (wu_ref, wu), (wd_ref, wd)))
    ]
    pl.semaphore_wait(barrier, greeted)

    shards = dims[0] * dims[1] * dims[2]

    def recv_sem(arr, p, at):
        return ag_recv.at[(arr * len(GATHER_PARTS) + p) * shards + index(at)]

    sends = {0: [], 1: []}
    slots = itertools.count()

    def shard(arr, p, at):
        start, size, _ = GATHER_PARTS[p]
        return bufs[arr].at[at[0], at[1], at[2], :, pl.ds(start * unit, size * unit)]

    def remote(arr, p, kid, slot, axis, by):
        at = origin(kid)
        target = moved(me, axis, by) if by else me
        ref = shard(arr, p, at)
        return pltpu.make_async_remote_copy(
            src_ref=ref, dst_ref=ref, send_sem=ag_send.at[slot], recv_sem=recv_sem(arr, p, at),
            device_id={"ha": index(target)}, device_id_type=MESH,
        )

    def forward(arr, p, kid, axis):
        if axis == 0:
            steps = [1, -1] if kid[0] == 0 else [-1 if kid[0] > 0 else 1]
        else:
            steps = range(1, dims[axis])
        for by in steps:
            slot = next(slots)
            conds = []
            if axis == 0:
                if dims[0] == 1:
                    continue
                conds = [on_line(by)]
            make = functools.partial(remote, arr, p, kid, slot, axis, by)
            when(conds, lambda: make().start())
            sends[arr].append((exists(kid) + conds, make))

    def handle(arr, p, kid):
        order = GATHER_PARTS[p][2]
        last = max((order.index(a) for a in range(3) if kid[a]), default=-1)

        def run():
            if last >= 0:
                remote(arr, p, kid, 0, 0, 0).wait_recv()
            for j, axis in enumerate(order):
                if j > last or (j == last and axis == 0):
                    forward(arr, p, kid, axis)

        when(exists(kid), run)

    line = [0] + [d for k in range(1, dims[0]) for d in (-k, k)]
    every = list(itertools.product(line, range(dims[1]), range(dims[2])))

    def kind(p, kid):
        order = GATHER_PARTS[p][2]
        last = max((order.index(a) for a in range(3) if kid[a]), default=-1)
        return last, abs(kid[0])

    def gather(arr, last, dist, line_last=None):
        for p, (_, _, order) in enumerate(GATHER_PARTS):
            if line_last is not None and line_last != (order[2] == 0):
                continue
            for kid in every:
                if kind(p, kid) == (last, dist):
                    handle(arr, p, kid)

    def gather_own(arr):
        own[arr].wait()
        gather(arr, -1, 0)

    def gather_begin(arr):
        gather(arr, 0, 0)
        gather(arr, 1, 0)
        for dist in range(1, dims[0]):
            gather(arr, 0, dist)
            if dist < dims[0] - 1:
                gather(arr, 1, dist)
            if dist > 1:
                gather(arr, 2, dist - 1, True)

    def gather_rest(arr):
        if dims[0] > 1:
            gather(arr, 1, dims[0] - 1)

    def gather_end(arr):
        for dist in range(dims[0]):
            gather(arr, 2, dist, False)
        if dims[0] > 1:
            gather(arr, 2, dims[0] - 1, True)

    depth = min(width, 2048)

    def project(which, weight):
        def block(i):
            cols = pl.ds(pl.multiple_of(i * depth, depth), depth)
            left = x_buf[:, :, :, :, cols].reshape(tokens, depth)
            return jnp.dot(left, weight[cols, :], preferred_element_type=F32)

        part[which] = block(0)

        @pl.loop(1, width // depth)
        def _(i):
            part[which] += block(i)

    def project_hidden():
        def block(i):
            cols = pl.ds(pl.multiple_of(i * depth, depth), depth)
            right = g_buf[:, :, :, :, cols].reshape(tokens, depth)
            return contract_cols(wd[:, cols], right)

        hid_t[...] = block(0)

        @pl.loop(1, width // depth)
        def _(i):
            hid_t[...] += block(i)

        part[2] = hid_t[...].T

    wa_copies = []

    def exchange(which):
        for by in range(1, cores):
            copy = pltpu.make_async_remote_copy(
                src_ref=part.at[which], dst_ref=wa_recv.at[by - 1, which],
                send_sem=wa_send.at[by - 1, which], recv_sem=wa_recv_sem.at[by - 1, which],
                device_id={"wa": lax.rem(core + by, cores)}, device_id_type=MESH,
            )
            copy.start()
            wa_copies.append(copy)

    gather_own(0)
    for load in loads:
        load.start()
    gather_begin(0)
    gather_own(1)
    gather_rest(0)
    gather_begin(1)
    gather_end(0)
    x_out = pltpu.make_async_copy(x_buf, xall_ref, copy_sem.at[0])
    x_out.start()
    loads[0].wait()
    project(0, wg)
    exchange(0)
    gather_rest(1)
    loads[1].wait()
    project(1, wu)
    exchange(1)
    gather_end(1)
    g_out = pltpu.make_async_copy(g_buf, gall_ref, copy_sem.at[1])
    g_out.start()
    loads[2].wait()
    project_hidden()
    exchange(2)
    x_out.wait()
    for conds, make in sends[0]:
        when(conds, lambda: make().wait_send())
    for copy in wa_copies:
        copy.wait()

    slab = 16

    @pl.loop(0, tokens // slab)
    def _(i):
        at = pl.ds(pl.multiple_of(i * slab, slab), slab)
        sums = []
        for which in range(3):
            total = part[which, at, :]
            for by in range(1, cores):
                total = total + wa_recv[by - 1, which, at, :]
            sums.append(total)
        hidden_ref[at, :], gg_ref[at, :], ug_ref[at, :] = pointwise(*sums)

    grads_t[0] = gg_ref[...].T
    grads_t[1] = ug_ref[...].T

    mine = x_buf
    rs_sends = []

    def spans(p):
        start, size, order = SUM_PARTS[p]
        return start * unit, size * unit, order

    def region(buf, p, order, stage, axis_pos):
        start, size, _ = spans(p)
        at = [slice(None)] * 3
        for a in order[:stage]:
            at[a] = me[a]
        at[order[stage]] = axis_pos
        return buf.at[at[0], at[1], at[2], :, pl.ds(start, size)]

    most = max(dims)

    def sum_send(p, stage):
        _, _, order = spans(p)
        axis = order[stage]
        for by in range(1, dims[axis]):
            there = moved(me, axis, by)
            sem = (p * 3 + stage) * most + by
            copy = pltpu.make_async_remote_copy(
                src_ref=region(mine, p, order, stage, there[axis]),
                dst_ref=region(rs_recv, p, order, stage, me[axis]),
                send_sem=rs_send.at[sem], recv_sem=rs_sem.at[sem],
                device_id={"ha": index(there)}, device_id_type=MESH,
            )
            copy.start()
            rs_sends.append(copy)

    def sum_take(p, stage):
        start, size, order = spans(p)
        axis = order[stage]
        froms = []
        for by in range(1, dims[axis]):
            source = moved(me, axis, -by)
            sem = (p * 3 + stage) * most + by
            ref = region(rs_recv, p, order, stage, source[axis])
            pltpu.make_async_remote_copy(
                src_ref=ref, dst_ref=ref, send_sem=rs_send.at[sem], recv_sem=rs_sem.at[sem],
                device_id={"ha": ha}, device_id_type=MESH,
            ).wait_recv()
            froms.append(source[axis])
        left = [a for a in range(3) if a not in order[: stage + 1]]
        count = 1
        for a in left:
            count *= dims[a]
        cols = pl.ds(start, size)

        def one(i):
            at = [None] * 3
            for a in order[: stage + 1]:
                at[a] = me[a]
            rest = i
            for a in reversed(left):
                at[a] = lax.rem(rest, dims[a])
                rest = lax.div(rest, dims[a])
            total = mine[at[0], at[1], at[2], :, cols].astype(F32)
            for source in froms:
                pos = list(at)
                pos[axis] = source
                total = total + rs_recv[pos[0], pos[1], pos[2], :, cols].astype(F32)
            if left:
                mine[at[0], at[1], at[2], :, cols] = total.astype(BF16)
            else:
                out_ref[:, cols] = total.astype(BF16)

        if left:
            pl.loop(0, count)(one)
        else:
            one(0)

    block = 4 * unit

    def compute(p):
        start, size, _ = SUM_PARTS[p]

        @pl.loop(start * unit // block, (start + size) * unit // block)
        def _(i):
            cols = pl.ds(pl.multiple_of(i * block, block), block)
            total = jnp.dot(wg[cols, :], grads_t[0], preferred_element_type=F32)
            total = total + jnp.dot(wu[cols, :], grads_t[1], preferred_element_type=F32)
            mine[:, :, :, :, cols] = total.astype(BF16).T.reshape(*dims, rows, block)

    def begin(wave):
        for p in SUM_WAVES[wave]:
            compute(p)
            sum_send(p, 0)

    def advance(wave, stage):
        for p in SUM_WAVES[wave]:
            sum_take(p, stage)
            if stage < 2:
                sum_send(p, stage + 1)

    waves = len(SUM_WAVES)
    begin(0)
    begin(1)
    for turn in range(waves + 1):
        if turn < waves:
            advance(turn, 0)
        if turn + 2 < waves:
            begin(turn + 2)
        if turn >= 1:
            advance(turn - 1, 1)
    for wave in range(waves):
        advance(wave, 2)
    for copy in rs_sends:
        copy.wait_send()
    for conds, make in sends[1]:
        when(conds, lambda: make().wait_send())
    g_out.wait()


def weight_kernel(factor, x_ref, g_ref, hidden_ref, gg_ref, ug_ref, dgate_ref, dup_ref, ddown_ref):
    tokens = hidden_ref.shape[0]
    x = x_ref[...].reshape(tokens, x_ref.shape[-1])
    g = g_ref[...].reshape(tokens, g_ref.shape[-1])
    dgate_ref[...] = (contract_rows(x, gg_ref[...]) * factor).astype(BF16)
    dup_ref[...] = (contract_rows(x, ug_ref[...]) * factor).astype(BF16)
    ddown_ref[...] = (contract_rows(hidden_ref[...], g) * factor).astype(BF16)


def weight_grads(x_all, g_all, hidden, gate_grad, up_grad, factor):
    lead, width = x_all.shape[:-1], x_all.shape[-1]
    tokens, ff = hidden.shape
    step = 512
    gathered = pl.BlockSpec((*lead, step), lambda i: (0, 0, 0, 0, i))
    whole = pl.BlockSpec((tokens, ff), lambda i: (0, 0))
    tall = pl.BlockSpec((step, ff), lambda i: (i, 0))
    return pl.pallas_call(
        functools.partial(weight_kernel, factor),
        grid=(width // step,),
        out_shape=(
            jax.ShapeDtypeStruct((width, ff), BF16),
            jax.ShapeDtypeStruct((width, ff), BF16),
            jax.ShapeDtypeStruct((ff, width), BF16),
        ),
        in_specs=[gathered, gathered, whole, whole, whole],
        out_specs=(tall, tall, pl.BlockSpec((ff, step), lambda i: (0, i))),
        compiler_params=pltpu.CompilerParams(vmem_limit_bytes=VMEM_LIMIT),
        cost_estimate=pl.CostEstimate(
            flops=6 * tokens * ff * width, bytes_accessed=2 * width * (3 * ff + 2 * tokens),
            transcendentals=0,
        ),
    )(x_all, g_all, hidden, gate_grad, up_grad)


def on_device(dims, cores, tokens, cotangent, gate_weight, up_weight, down_weight):
    rows, width = tokens.shape
    ff = gate_weight.shape[1]
    count = rows * dims[0] * dims[1] * dims[2]
    shards = dims[0] * dims[1] * dims[2]
    gathered = (*dims, rows, width)
    hbm = pl.BlockSpec(memory_space=pl.ANY)
    vmem = pl.BlockSpec(memory_space=pltpu.VMEM)
    dma = pltpu.SemaphoreType.DMA
    ag_count = 2 * len(GATHER_PARTS) * shards
    rs_count = 3 * len(SUM_PARTS) * max(dims)
    others = max(cores - 1, 1)
    x_all, g_all, hidden, gate_grad, up_grad, input_grad = pl.pallas_call(
        functools.partial(main_kernel, dims, cores),
        out_shape=(
            jax.ShapeDtypeStruct(gathered, BF16),
            jax.ShapeDtypeStruct(gathered, BF16),
            jax.ShapeDtypeStruct((count, ff), BF16),
            jax.ShapeDtypeStruct((count, ff), BF16),
            jax.ShapeDtypeStruct((count, ff), BF16),
            jax.ShapeDtypeStruct((rows, width), BF16),
        ),
        in_specs=[hbm] * 5,
        out_specs=(hbm, hbm, vmem, vmem, vmem, vmem),
        scratch_shapes=[
            pltpu.VMEM(gathered, BF16),
            pltpu.VMEM(gathered, BF16),
            pltpu.VMEM((width, ff), BF16),
            pltpu.VMEM((width, ff), BF16),
            pltpu.VMEM((ff, width), BF16),
            pltpu.VMEM((3, count, ff), F32),
            pltpu.VMEM((others, 3, count, ff), F32),
            pltpu.VMEM(gathered, BF16),
            pltpu.VMEM((ff, count), F32),
            pltpu.VMEM((2, ff, count), BF16),
            dma((2,)), dma((3,)), dma((2,)),
            dma((2 * ag_count,)), dma((ag_count,)),
            dma((others, 3)), dma((others, 3)),
            dma((rs_count,)), dma((rs_count,)),
        ],
        compiler_params=pltpu.CompilerParams(
            collective_id=0, has_side_effects=True, vmem_limit_bytes=VMEM_LIMIT
        ),
        cost_estimate=pl.CostEstimate(
            flops=10 * count * ff * width, bytes_accessed=2 * width * (3 * ff + 2 * count),
            transcendentals=count * ff,
        ),
    )(tokens, cotangent, gate_weight, up_weight, down_weight)
    grads = weight_grads(x_all, g_all, hidden, gate_grad, up_grad, count ** (-0.5))
    return (input_grad, *grads)


def on_device_plain(tokens, cotangent, gate_weight, up_weight, down_weight):
    inputs_all = lax.all_gather(tokens, "ha", axis=0, tiled=True)
    grads_all = lax.all_gather(cotangent, "ha", axis=0, tiled=True)
    factor = inputs_all.shape[0] ** (-0.5)
    gate_part = jnp.dot(inputs_all, gate_weight, preferred_element_type=F32)
    up_part = jnp.dot(inputs_all, up_weight, preferred_element_type=F32)
    hidden_part = contract_cols(grads_all, down_weight)
    gate_sum, up_sum, hidden_grad = lax.psum((gate_part, up_part, hidden_part), "wa")
    hidden, gate_grad, up_grad = pointwise(gate_sum, up_sum, hidden_grad)
    down_weight_grad = (contract_rows(hidden, grads_all) * factor).astype(BF16)
    gate_weight_grad = (contract_rows(inputs_all, gate_grad) * factor).astype(BF16)
    up_weight_grad = (contract_rows(inputs_all, up_grad) * factor).astype(BF16)
    input_grad = lax.psum_scatter(
        contract_cols(gate_grad, gate_weight) + contract_cols(up_grad, up_weight),
        "ha", scatter_dimension=0, tiled=True,
    )
    return (input_grad.astype(BF16), gate_weight_grad, up_weight_grad, down_weight_grad)


def fits(dims, cores, rows, width, ff):
    count = dims[0] * dims[1] * dims[2] * rows
    held = 6 * count * width + 6 * width * ff + 12 * cores * count * ff + 6 * count * ff
    return rows % 16 == 0 and width % 2048 == 0 and ff % 128 == 0 and held < VMEM_LIMIT


def solution(mesh):
    placed = (P("ha", "wa"), P("ha", "wa"), P("wa", "ha"), P("wa", "ha"), P("ha", "wa"))
    cores, along = mesh.shape["wa"], mesh.shape["ha"]
    dims = (along // 4, 2, 2) if along % 4 == 0 else (along, 1, 1)

    def body(tokens, cotangent, gate_weight, up_weight, down_weight):
        plan = on_device_plain
        if fits(dims, cores, *tokens.shape, gate_weight.shape[1]):
            plan = functools.partial(on_device, dims, cores)
        return plan(tokens, cotangent, gate_weight, up_weight, down_weight)

    return jax.shard_map(
        body,
        mesh=mesh,
        in_specs=placed,
        out_specs=(P("ha", "wa"), P("wa", "ha"), P("wa", "ha"), P("ha", "wa")),
        check_vma=False,
    )
```

```python
import functools
import itertools

import jax
import jax.numpy as jnp
from jax import lax
from jax.experimental import pallas as pl
from jax.experimental.pallas import tpu as pltpu
from jax.sharding import PartitionSpec as P

MESH = pl.DeviceIdType.MESH
BF16, F32 = jnp.bfloat16, jnp.float32
VMEM_LIMIT = 61 * 1024 * 1024

GATHER_PARTS = ((0, 7, (0, 1, 2)), (7, 7, (0, 2, 1)), (14, 1, (2, 1, 0)), (15, 1, (1, 2, 0)))
SUM_PARTS = (
    (0, 4, (2, 1, 0)),
    (7, 4, (1, 2, 0)),
    (14, 1, (0, 1, 2)),
    (15, 1, (0, 2, 1)),
    (4, 3, (2, 1, 0)),
    (11, 3, (1, 2, 0)),
)


def pointwise(gate_sum, up_sum, hidden_grad):
    sigma = jax.nn.sigmoid(gate_sum)
    hidden = (gate_sum * sigma * up_sum).astype(BF16)
    gate_grad = (hidden_grad * up_sum * sigma * (1.0 + gate_sum * (1.0 - sigma))).astype(BF16)
    up_grad = (hidden_grad * gate_sum * sigma).astype(BF16)
    return (hidden, gate_grad, up_grad)


def contract_rows(left, right):
    return lax.dot_general(left, right, (((0,), (0,)), ((), ())), preferred_element_type=F32)


def contract_cols(left, right):
    return lax.dot_general(left, right, (((1,), (1,)), ((), ())), preferred_element_type=F32)


def main_kernel(
    dims, cores,
    tok_ref, cot_ref, wg_ref, wu_ref, wd_ref,
    xall_ref, gall_ref, hidden_ref, gg_ref, ug_ref, out_ref,
    x_buf, g_buf, wg, wu, wd, part, wa_recv, rs_recv, hid_t, grads_t,
    in_sem, w_sem, copy_sem, ag_send, ag_recv, wa_send, wa_recv_sem, rs_send, rs_sem,
):
    rows, width = tok_ref.shape
    ff = wg_ref.shape[1]
    tokens = rows * dims[0] * dims[1] * dims[2]
    unit = width // 16
    ha = lax.axis_index("ha")
    core = lax.axis_index("wa")
    me = (
        lax.div(ha, dims[1] * dims[2]),
        lax.rem(lax.div(ha, dims[2]), dims[1]),
        lax.rem(ha, dims[2]),
    )

    def moved(at, axis, by):
        pos = list(at)
        pos[axis] = lax.rem(at[axis] + by + dims[axis], dims[axis])
        return tuple(pos)

    def index(at):
        return (at[0] * dims[1] + at[1]) * dims[2] + at[2]

    def origin(kid):
        return tuple(lax.rem(me[a] - kid[a] + dims[a], dims[a]) for a in range(3))

    barrier = pltpu.get_barrier_semaphore()
    greeted = 0
    for axis in range(3):
        for by in range(1, dims[axis]):
            pl.semaphore_signal(
                barrier, inc=1, device_id={"ha": index(moved(me, axis, by))}, device_id_type=MESH
            )
            greeted += 1
    for by in range(1, cores):
        pl.semaphore_signal(
            barrier, inc=1, device_id={"wa": lax.rem(core + by, cores)}, device_id_type=MESH
        )
        greeted += 1

    bufs = (x_buf, g_buf)
    own = [
        pltpu.make_async_copy(ref, buf.at[me[0], me[1], me[2]], in_sem.at[i])
        for i, (ref, buf) in enumerate(((tok_ref, x_buf), (cot_ref, g_buf)))
    ]
    for copy in own:
        copy.start()
    loads = [
        pltpu.make_async_copy(ref, buf, w_sem.at[i])
        for i, (ref, buf) in enumerate(((wg_ref, wg), (wu_ref, wu), (wd_ref, wd)))
    ]
    pl.semaphore_wait(barrier, greeted)

    def sem_id(arr, p, kid):
        return ((arr * len(GATHER_PARTS) + p) * dims[0] + kid[0]) * dims[1] * dims[2] + (
            kid[1] * dims[2] + kid[2]
        )

    sends = {0: [], 1: []}

    def shard(arr, p, kid):
        start, size, _ = GATHER_PARTS[p]
        at = origin(kid)
        return bufs[arr].at[at[0], at[1], at[2], :, pl.ds(start * unit, size * unit)]

    def forward(arr, p, kid, axis):
        for by in range(1, dims[axis]):
            there = list(kid)
            there[axis] += by
            ref = shard(arr, p, kid)
            copy = pltpu.make_async_remote_copy(
                src_ref=ref, dst_ref=ref,
                send_sem=ag_send.at[sem_id(arr, p, there)],
                recv_sem=ag_recv.at[sem_id(arr, p, there)],
                device_id={"ha": index(moved(me, axis, by))}, device_id_type=MESH,
            )
            copy.start()
            sends[arr].append(copy)

    def arrived(arr, p, kid):
        ref = shard(arr, p, kid)
        pltpu.make_async_remote_copy(
            src_ref=ref, dst_ref=ref,
            send_sem=ag_send.at[sem_id(arr, p, kid)], recv_sem=ag_recv.at[sem_id(arr, p, kid)],
            device_id={"ha": ha}, device_id_type=MESH,
        ).wait_recv()

    every = list(itertools.product(*(range(n) for n in dims)))

    def gather_stage(arr, stage):
        if stage == 0:
            own[arr].wait()
        for p, (_, _, order) in enumerate(GATHER_PARTS):
            for kid in every:
                if stage == 0:
                    take = not any(kid)
                else:
                    take = kid[order[stage - 1]] and not any(kid[a] for a in order[stage:])
                if not take:
                    continue
                if stage:
                    arrived(arr, p, kid)
                for axis in order[stage:]:
                    forward(arr, p, kid, axis)

    depth = min(width, 2048)

    def project(which, weight):
        def block(i):
            cols = pl.ds(pl.multiple_of(i * depth, depth), depth)
            left = x_buf[:, :, :, :, cols].reshape(tokens, depth)
            return jnp.dot(left, weight[cols, :], preferred_element_type=F32)

        part[which] = block(0)

        @pl.loop(1, width // depth)
        def _(i):
            part[which] += block(i)

    def project_hidden():
        def block(i):
            cols = pl.ds(pl.multiple_of(i * depth, depth), depth)
            right = g_buf[:, :, :, :, cols].reshape(tokens, depth)
            return contract_cols(wd[:, cols], right)

        hid_t[...] = block(0)

        @pl.loop(1, width // depth)
        def _(i):
            hid_t[...] += block(i)

        part[2] = hid_t[...].T

    wa_copies = []

    def exchange(which):
        for by in range(1, cores):
            copy = pltpu.make_async_remote_copy(
                src_ref=part.at[which], dst_ref=wa_recv.at[by - 1, which],
                send_sem=wa_send.at[by - 1, which], recv_sem=wa_recv_sem.at[by - 1, which],
                device_id={"wa": lax.rem(core + by, cores)}, device_id_type=MESH,
            )
            copy.start()
            wa_copies.append(copy)

    gather_stage(0, 0)
    for load in loads:
        load.start()
    gather_stage(0, 1)
    gather_stage(1, 0)
    gather_stage(0, 2)
    gather_stage(1, 1)
    gather_stage(0, 3)
    x_out = pltpu.make_async_copy(x_buf, xall_ref, copy_sem.at[0])
    x_out.start()
    loads[0].wait()
    project(0, wg)
    exchange(0)
    gather_stage(1, 2)
    loads[1].wait()
    project(1, wu)
    exchange(1)
    gather_stage(1, 3)
    g_out = pltpu.make_async_copy(g_buf, gall_ref, copy_sem.at[1])
    g_out.start()
    loads[2].wait()
    project_hidden()
    exchange(2)
    x_out.wait()
    for copy in sends[0]:
        copy.wait_send()
    for copy in wa_copies:
        copy.wait()

    slab = 16

    @pl.loop(0, tokens // slab)
    def _(i):
        at = pl.ds(pl.multiple_of(i * slab, slab), slab)
        sums = []
        for which in range(3):
            total = part[which, at, :]
            for by in range(1, cores):
                total = total + wa_recv[by - 1, which, at, :]
            sums.append(total)
        hidden_ref[at, :], gg_ref[at, :], ug_ref[at, :] = pointwise(*sums)

    grads_t[0] = gg_ref[...].T
    grads_t[1] = ug_ref[...].T

    mine = x_buf
    rs_sends = []

    def spans(p):
        start, size, order = SUM_PARTS[p]
        return start * unit, size * unit, order

    def region(buf, p, order, stage, axis_pos):
        start, size, _ = spans(p)
        at = [slice(None)] * 3
        for a in order[:stage]:
            at[a] = me[a]
        at[order[stage]] = axis_pos
        return buf.at[at[0], at[1], at[2], :, pl.ds(start, size)]

    most = max(dims)

    def sum_send(p, stage):
        _, _, order = spans(p)
        axis = order[stage]
        for by in range(1, dims[axis]):
            there = moved(me, axis, by)
            sem = (p * 3 + stage) * most + by
            copy = pltpu.make_async_remote_copy(
                src_ref=region(mine, p, order, stage, there[axis]),
                dst_ref=region(rs_recv, p, order, stage, me[axis]),
                send_sem=rs_send.at[sem], recv_sem=rs_sem.at[sem],
                device_id={"ha": index(there)}, device_id_type=MESH,
            )
            copy.start()
            rs_sends.append(copy)

    def sum_take(p, stage):
        start, size, order = spans(p)
        axis = order[stage]
        froms = []
        for by in range(1, dims[axis]):
            source = moved(me, axis, -by)
            sem = (p * 3 + stage) * most + by
            ref = region(rs_recv, p, order, stage, source[axis])
            pltpu.make_async_remote_copy(
                src_ref=ref, dst_ref=ref, send_sem=rs_send.at[sem], recv_sem=rs_sem.at[sem],
                device_id={"ha": ha}, device_id_type=MESH,
            ).wait_recv()
            froms.append(source[axis])
        left = [a for a in range(3) if a not in order[: stage + 1]]
        count = 1
        for a in left:
            count *= dims[a]
        cols = pl.ds(start, size)

        def one(i):
            at = [None] * 3
            for a in order[: stage + 1]:
                at[a] = me[a]
            rest = i
            for a in reversed(left):
                at[a] = lax.rem(rest, dims[a])
                rest = lax.div(rest, dims[a])
            total = mine[at[0], at[1], at[2], :, cols].astype(F32)
            for source in froms:
                pos = list(at)
                pos[axis] = source
                total = total + rs_recv[pos[0], pos[1], pos[2], :, cols].astype(F32)
            if left:
                mine[at[0], at[1], at[2], :, cols] = total.astype(BF16)
            else:
                out_ref[:, cols] = total.astype(BF16)

        if left:
            pl.loop(0, count)(one)
        else:
            one(0)

    for p in range(len(SUM_PARTS)):
        start, size, _ = SUM_PARTS[p]

        @pl.loop(start, start + size)
        def _(i):
            cols = pl.ds(pl.multiple_of(i * unit, unit), unit)
            total = jnp.dot(wg[cols, :], grads_t[0], preferred_element_type=F32)
            total = total + jnp.dot(wu[cols, :], grads_t[1], preferred_element_type=F32)
            mine[:, :, :, :, cols] = total.astype(BF16).T.reshape(*dims, rows, unit)

        sum_send(p, 0)
    for stage in range(3):
        for p in range(len(SUM_PARTS)):
            sum_take(p, stage)
            if stage < 2:
                sum_send(p, stage + 1)
    for copy in rs_sends + sends[1]:
        copy.wait_send()
    g_out.wait()


def weight_kernel(factor, x_ref, g_ref, hidden_ref, gg_ref, ug_ref, dgate_ref, dup_ref, ddown_ref):
    tokens = hidden_ref.shape[0]
    x = x_ref[...].reshape(tokens, x_ref.shape[-1])
    g = g_ref[...].reshape(tokens, g_ref.shape[-1])
    dgate_ref[...] = (contract_rows(x, gg_ref[...]) * factor).astype(BF16)
    dup_ref[...] = (contract_rows(x, ug_ref[...]) * factor).astype(BF16)
    ddown_ref[...] = (contract_rows(hidden_ref[...], g) * factor).astype(BF16)


def weight_grads(x_all, g_all, hidden, gate_grad, up_grad, factor):
    lead, width = x_all.shape[:-1], x_all.shape[-1]
    tokens, ff = hidden.shape
    step = 512
    gathered = pl.BlockSpec((*lead, step), lambda i: (0, 0, 0, 0, i))
    whole = pl.BlockSpec((tokens, ff), lambda i: (0, 0))
    tall = pl.BlockSpec((step, ff), lambda i: (i, 0))
    return pl.pallas_call(
        functools.partial(weight_kernel, factor),
        grid=(width // step,),
        out_shape=(
            jax.ShapeDtypeStruct((width, ff), BF16),
            jax.ShapeDtypeStruct((width, ff), BF16),
            jax.ShapeDtypeStruct((ff, width), BF16),
        ),
        in_specs=[gathered, gathered, whole, whole, whole],
        out_specs=(tall, tall, pl.BlockSpec((ff, step), lambda i: (0, i))),
        compiler_params=pltpu.CompilerParams(vmem_limit_bytes=VMEM_LIMIT),
        cost_estimate=pl.CostEstimate(
            flops=6 * tokens * ff * width, bytes_accessed=2 * width * (3 * ff + 2 * tokens),
            transcendentals=0,
        ),
    )(x_all, g_all, hidden, gate_grad, up_grad)


def on_device(dims, cores, tokens, cotangent, gate_weight, up_weight, down_weight):
    rows, width = tokens.shape
    ff = gate_weight.shape[1]
    count = rows * dims[0] * dims[1] * dims[2]
    shards = dims[0] * dims[1] * dims[2]
    gathered = (*dims, rows, width)
    hbm = pl.BlockSpec(memory_space=pl.ANY)
    vmem = pl.BlockSpec(memory_space=pltpu.VMEM)
    dma = pltpu.SemaphoreType.DMA
    ag_count = 2 * len(GATHER_PARTS) * shards
    rs_count = 3 * len(SUM_PARTS) * max(dims)
    others = max(cores - 1, 1)
    x_all, g_all, hidden, gate_grad, up_grad, input_grad = pl.pallas_call(
        functools.partial(main_kernel, dims, cores),
        out_shape=(
            jax.ShapeDtypeStruct(gathered, BF16),
            jax.ShapeDtypeStruct(gathered, BF16),
            jax.ShapeDtypeStruct((count, ff), BF16),
            jax.ShapeDtypeStruct((count, ff), BF16),
            jax.ShapeDtypeStruct((count, ff), BF16),
            jax.ShapeDtypeStruct((rows, width), BF16),
        ),
        in_specs=[hbm] * 5,
        out_specs=(hbm, hbm, vmem, vmem, vmem, vmem),
        scratch_shapes=[
            pltpu.VMEM(gathered, BF16),
            pltpu.VMEM(gathered, BF16),
            pltpu.VMEM((width, ff), BF16),
            pltpu.VMEM((width, ff), BF16),
            pltpu.VMEM((ff, width), BF16),
            pltpu.VMEM((3, count, ff), F32),
            pltpu.VMEM((others, 3, count, ff), F32),
            pltpu.VMEM(gathered, BF16),
            pltpu.VMEM((ff, count), F32),
            pltpu.VMEM((2, ff, count), BF16),
            dma((2,)), dma((3,)), dma((2,)),
            dma((ag_count,)), dma((ag_count,)),
            dma((others, 3)), dma((others, 3)),
            dma((rs_count,)), dma((rs_count,)),
        ],
        compiler_params=pltpu.CompilerParams(
            collective_id=0, has_side_effects=True, vmem_limit_bytes=VMEM_LIMIT
        ),
        cost_estimate=pl.CostEstimate(
            flops=10 * count * ff * width, bytes_accessed=2 * width * (3 * ff + 2 * count),
            transcendentals=count * ff,
        ),
    )(tokens, cotangent, gate_weight, up_weight, down_weight)
    grads = weight_grads(x_all, g_all, hidden, gate_grad, up_grad, count ** (-0.5))
    return (input_grad, *grads)


def on_device_plain(tokens, cotangent, gate_weight, up_weight, down_weight):
    inputs_all = lax.all_gather(tokens, "ha", axis=0, tiled=True)
    grads_all = lax.all_gather(cotangent, "ha", axis=0, tiled=True)
    factor = inputs_all.shape[0] ** (-0.5)
    gate_part = jnp.dot(inputs_all, gate_weight, preferred_element_type=F32)
    up_part = jnp.dot(inputs_all, up_weight, preferred_element_type=F32)
    hidden_part = contract_cols(grads_all, down_weight)
    gate_sum, up_sum, hidden_grad = lax.psum((gate_part, up_part, hidden_part), "wa")
    hidden, gate_grad, up_grad = pointwise(gate_sum, up_sum, hidden_grad)
    down_weight_grad = (contract_rows(hidden, grads_all) * factor).astype(BF16)
    gate_weight_grad = (contract_rows(inputs_all, gate_grad) * factor).astype(BF16)
    up_weight_grad = (contract_rows(inputs_all, up_grad) * factor).astype(BF16)
    input_grad = lax.psum_scatter(
        contract_cols(gate_grad, gate_weight) + contract_cols(up_grad, up_weight),
        "ha", scatter_dimension=0, tiled=True,
    )
    return (input_grad.astype(BF16), gate_weight_grad, up_weight_grad, down_weight_grad)


def fits(dims, cores, rows, width, ff):
    count = dims[0] * dims[1] * dims[2] * rows
    held = 6 * count * width + 6 * width * ff + 12 * cores * count * ff + 6 * count * ff
    return rows % 16 == 0 and width % 2048 == 0 and ff % 128 == 0 and held < VMEM_LIMIT


def solution(mesh):
    placed = (P("ha", "wa"), P("ha", "wa"), P("wa", "ha"), P("wa", "ha"), P("ha", "wa"))
    cores, along = mesh.shape["wa"], mesh.shape["ha"]
    dims = (along // 4, 2, 2) if along % 4 == 0 else (along, 1, 1)

    def body(tokens, cotangent, gate_weight, up_weight, down_weight):
        plan = on_device_plain
        if fits(dims, cores, *tokens.shape, gate_weight.shape[1]):
            plan = functools.partial(on_device, dims, cores)
        return plan(tokens, cotangent, gate_weight, up_weight, down_weight)

    return jax.shard_map(
        body,
        mesh=mesh,
        in_specs=placed,
        out_specs=(P("ha", "wa"), P("wa", "ha"), P("wa", "ha"), P("ha", "wa")),
        check_vma=False,
    )
```
